32 devices in a mesh: row: 4 (over y, x), col: 8 (over z, core).
Axes of the slice: x: 2, y: 2, z: 4, core: 2. Of those that a mesh axis runs over, the one named last changes fastest.
Arguments:
- latents: bfloat16 [128, 128, 512], P('row', 'col'), may hold values from -6 to 6
- cotangent: bfloat16 [128, 128, 512], P('row', 'col'), may hold values from -6 to 6
- w_row: bfloat16 [4, 512, 512], replicated, may hold values from -6.6733202 to 6.6733202, as said below
- w_col: bfloat16 [4, 512, 512], replicated, may hold values from -6.6733202 to 6.6733202, as said below
- keep_heads: int32 [2, 8], replicated, may hold values 0 or 1
Outputs:
- output: bfloat16 [128, 128, 512], P('row', 'col')
- grad_latents: bfloat16 [128, 128, 512], P('row', 'col')
- grad_row: float32 [4, 512, 512], replicated
- grad_col: float32 [4, 512, 512], replicated
The draws below stay inside these ranges and needn't reach their ends.
Inputs may be any that keep to these rules, and one draw needn't show every extreme that they name: `w_row`: projection weights. `w_col`: projection weights.
All inputs are finite; a program needn't handle non-finite values.
Results may differ from the reference program's by a relative error of at most 0.033.
Values may be sent and summed in bfloat16 or wider, within the bound.
A program may use at most 128 MiB of HBM per device.

```python
import jax
import jax.numpy as jnp
from jax import lax

HEADS = 8
HEAD = 64
D = 512
RT = 32
CT = 16
GH = 128
GW = 128
N_ROW = 4
N_COL = 8


def stacked_weights(key, salt):
    base_key = jax.random.fold_in(key, salt)
    normal_part = jnp.clip(jax.random.normal(base_key, (4, D, D), jnp.float32), -5.0, 5.0) * D ** (-0.5)
    return normal_part.astype(jnp.bfloat16)


def draw_w_row(key, part):
    return stacked_weights(key, 11)


def draw_w_col(key, part):
    return stacked_weights(key, 23)


def touch_ends(values, stream_key, low, largest):
    longest = values.shape.index(max(values.shape))
    spots = []
    for shift in (0, 1):
        where = [jax.random.randint(jax.random.fold_in(stream_key, axis), (), 0, length) for axis, length in enumerate(values.shape)]
        where[longest] = (where[longest] + shift) % values.shape[longest]
        spots.append(tuple(where))
    return values.at[spots[0]].set(low).at[spots[1]].set(largest)


def shard_levels(key, extent, shards, smallest, high):
    def one(position, parts):
        steps = jax.random.uniform(jax.random.fold_in(jax.random.fold_in(key, 6), position), (parts,), jnp.float32, smallest / len(shards), high / len(shards))
        return jnp.repeat(jnp.exp(steps), extent[position] // parts).reshape((-1,) + (1,) * (len(extent) - position - 1))

    factor_of = one(*shards[0])
    for cut in shards[1:]:
        factor_of = factor_of * one(*cut)
    return factor_of


def normal_values(stream_key, extent, deviation, most, pieces=(), kind=jnp.bfloat16):
    factor_of = shard_levels(stream_key, extent, pieces, -0.22, 0.18) if pieces else 1.0
    values = jax.random.normal(stream_key, extent, jnp.float32) * deviation * factor_of
    return jnp.minimum(jnp.maximum(values, -most), most).astype(kind)


def setup_inputs(seed: int = 0) -> dict:
    arg_keys = jax.random.split(jax.random.key(seed), 6)
    latents = normal_values(arg_keys[0], (GH, GW, D), 1.0, 6.0, ((0, 4), (1, 8)))
    cotangent = normal_values(arg_keys[1], (GH, GW, D), 1.0, 6.0, ((0, 4), (1, 8)))
    w_row = draw_w_row(jax.random.fold_in(arg_keys[5], 71), 0)
    w_col = draw_w_col(jax.random.fold_in(arg_keys[5], 71), 0)
    keep_heads = touch_ends((jax.random.randint(arg_keys[4], (2, HEADS), 0, 4) < 3).astype(jnp.int32), jax.random.fold_in(arg_keys[4], 1), 0, 1)
    return {"latents": latents, "cotangent": cotangent, "w_row": w_row, "w_col": w_col, "keep_heads": keep_heads}


EPSILON = 1e-06

def mat_tn(left, right):
    return lax.dot_general(left, right, (((0,), (0,)), ((), ())), preferred_element_type=jnp.float32)

def mat_nt(left, right):
    return lax.dot_general(left, right, (((1,), (1,)), ((), ())), preferred_element_type=jnp.float32)

def head_specs(letters):
    if letters == 'nl':
        return ('nlhe', 'nmhe')
    return ('lnhe', 'mnhe')

def line_forward(inputs, weights, head_gain, letters):
    in_shape = inputs.shape
    model_width = in_shape[2]
    q_spec, k_spec = head_specs(letters)
    values_f = inputs.astype(jnp.float32)
    inv_rms = lax.rsqrt(lax.optimization_barrier(jnp.mean(values_f * values_f, axis=-1, keepdims=True)) + EPSILON)
    normed = (values_f * inv_rms).astype(jnp.bfloat16).reshape(-1, model_width)

    def project(which_proj):
        result = jnp.dot(normed, weights[which_proj], preferred_element_type=jnp.float32)
        return result.astype(jnp.bfloat16).reshape(in_shape[0], in_shape[1], HEADS, HEAD)
    q_proj, k_proj, v_proj = (project(0), project(1), project(2))
    scores = jnp.einsum(q_spec + ',' + k_spec + '->nhlm', q_proj, k_proj, preferred_element_type=jnp.float32) * HEAD ** (-0.5)
    row_max = lax.optimization_barrier(jnp.max(scores, axis=-1, keepdims=True))
    exp_scores = jnp.exp(scores - row_max)
    attn_probs = exp_scores / lax.optimization_barrier(jnp.sum(exp_scores, axis=-1, keepdims=True))
    probs_low = attn_probs.astype(jnp.bfloat16)
    mixed_heads = jnp.einsum('nhlm,' + k_spec + '->' + q_spec, probs_low, v_proj, preferred_element_type=jnp.float32)
    attended = (mixed_heads * head_gain[:, None]).astype(jnp.bfloat16).reshape(-1, model_width)
    result = values_f + jnp.dot(attended, weights[3], preferred_element_type=jnp.float32).reshape(in_shape)
    saved_state = (normed, q_proj, k_proj, v_proj, attn_probs, probs_low, attended, inv_rms)
    return (result.astype(jnp.bfloat16), saved_state)

def line_backward(grad_out, inputs, saved_state, weights, head_gain, letters):
    normed, q_proj, k_proj, v_proj, attn_probs, probs_low, attended, inv_rms = saved_state
    in_shape = inputs.shape
    model_width = in_shape[2]
    q_spec, k_spec = head_specs(letters)
    grad_flat = grad_out.reshape(-1, model_width)
    grad_wo = mat_tn(attended, grad_flat)
    grad_att = mat_nt(grad_flat, weights[3]).reshape(in_shape[0], in_shape[1], HEADS, HEAD)
    grad_att = (grad_att * head_gain[:, None]).astype(jnp.bfloat16)
    grad_probs = jnp.einsum(q_spec + ',' + k_spec + '->nhlm', grad_att, v_proj, preferred_element_type=jnp.float32)
    grad_scores = attn_probs * (grad_probs - lax.optimization_barrier(jnp.sum(attn_probs * grad_probs, axis=-1, keepdims=True))) * HEAD ** (-0.5)
    grad_scores = grad_scores.astype(jnp.bfloat16)
    grad_q = jnp.einsum('nhlm,' + k_spec + '->' + q_spec, grad_scores, k_proj, preferred_element_type=jnp.float32)
    grad_k = jnp.einsum('nhlm,' + q_spec + '->' + k_spec, grad_scores, q_proj, preferred_element_type=jnp.float32)
    grad_v = jnp.einsum('nhlm,' + q_spec + '->' + k_spec, probs_low, grad_att, preferred_element_type=jnp.float32)
    grad_q = grad_q.astype(jnp.bfloat16).reshape(-1, model_width)
    grad_k = grad_k.astype(jnp.bfloat16).reshape(-1, model_width)
    grad_v = grad_v.astype(jnp.bfloat16).reshape(-1, model_width)
    grad_weights = jnp.stack([mat_tn(normed, grad_q), mat_tn(normed, grad_k), mat_tn(normed, grad_v), grad_wo])
    grad_normed = mat_nt(grad_q, weights[0]) + mat_nt(grad_k, weights[1]) + mat_nt(grad_v, weights[2])
    values_f = inputs.astype(jnp.float32).reshape(-1, model_width)
    inv_flat = inv_rms.reshape(-1, 1)
    grad_in = grad_flat.astype(jnp.float32) + inv_flat * grad_normed
    grad_in = grad_in - values_f * inv_flat * inv_flat * inv_flat * lax.optimization_barrier(jnp.mean(grad_normed * values_f, axis=-1, keepdims=True))
    return (grad_in.astype(jnp.bfloat16).reshape(in_shape), grad_weights)

def reference(latents, cotangent, w_row, w_col, keep_heads):
    head_gain = keep_heads.astype(jnp.float32)
    rows_group = RT // N_COL
    cols_group = CT // N_ROW
    grid_rows, grid_cols, model_width = latents.shape
    row_blocks = latents.reshape(grid_rows // rows_group, rows_group, grid_cols, model_width)

    def row_forward(line_block):
        return line_forward(line_block, w_row, head_gain[0], 'nl')[0]
    mid_rows = lax.map(row_forward, row_blocks).reshape(grid_rows, grid_cols, model_width)
    col_blocks = mid_rows.reshape(grid_rows, grid_cols // cols_group, cols_group, model_width).transpose(1, 0, 2, 3)
    grad_blocks = cotangent.reshape(grid_rows, grid_cols // cols_group, cols_group, model_width).transpose(1, 0, 2, 3)
    zero_grads = jnp.zeros((4, model_width, model_width), jnp.float32)

    def col_step(totals, inputs_pair):
        line_block, grad_block = inputs_pair
        result, saved_state = line_forward(line_block, w_col, head_gain[1], 'ln')
        grad_in, grad_weights = line_backward(grad_block, line_block, saved_state, w_col, head_gain[1], 'ln')
        return (totals + grad_weights, (result, grad_in))
    grad_col, (col_outs, col_grads) = lax.scan(col_step, zero_grads, (col_blocks, grad_blocks))
    output = col_outs.transpose(1, 0, 2, 3).reshape(grid_rows, grid_cols, model_width)
    grad_mid = col_grads.transpose(1, 0, 2, 3).reshape(grid_rows // rows_group, rows_group, grid_cols, model_width)

    def row_step(totals, inputs_pair):
        line_block, grad_block = inputs_pair
        result, saved_state = line_forward(line_block, w_row, head_gain[0], 'nl')
        grad_in, grad_weights = line_backward(grad_block, line_block, saved_state, w_row, head_gain[0], 'nl')
        return (totals + grad_weights, grad_in)
    grad_row, row_grads = lax.scan(row_step, zero_grads, (row_blocks, grad_mid))
    grad_latents = row_grads.reshape(grid_rows, grid_cols, model_width)
    return (output, grad_latents, grad_row, grad_col)
```

```python
import functools

import jax
import jax.numpy as jnp
from jax import lax
from jax.experimental import pallas as pl
from jax.experimental.pallas import tpu as pltpu
from jax.sharding import PartitionSpec as P

HEADS = 8
HEAD = 64
EPSILON = 1e-06
BF = jnp.bfloat16
F32 = jnp.float32


def dot(left, right, ca=1, cb=0):
    return lax.dot_general(
        left, right, (((ca,), (cb,)), ((), ())), preferred_element_type=F32
    )


def reorder(rows, sizes, order):
    total = rows.shape[0]
    index = lax.broadcasted_iota(jnp.int32, (total, 1), 0)
    strides, stride = [0] * len(sizes), 1
    for axis in reversed(range(len(sizes))):
        strides[axis], stride = stride, stride * sizes[axis]
    source, stride = jnp.zeros_like(index), 1
    for axis in reversed(order):
        digit = lax.rem(lax.div(index, jnp.int32(stride)), jnp.int32(sizes[axis]))
        source = source + digit * strides[axis]
        stride *= sizes[axis]
    column = lax.broadcasted_iota(jnp.int32, (total, total), 1)
    matrix = jnp.where(column == source, 1.0, 0.0).astype(BF)
    return dot(matrix, rows).astype(BF)


def inverse_rms(values):
    return lax.rsqrt(jnp.mean(values * values, axis=-1, keepdims=True) + EPSILON)


def halves(pair, first):
    zero = jnp.zeros_like(pair)
    return jnp.concatenate([jnp.where(first, pair, zero), jnp.where(first, zero, pair)], axis=0)


def attention(lines, q_ref, k_ref, v_ref, a_ref, da_ref, dq_ref, dk_ref, dv_ref, gain_ref):
    length = q_ref.shape[0] // lines
    wide = 2 * HEAD
    first = lax.broadcasted_iota(jnp.int32, (length, wide), 1) < HEAD
    scale = HEAD ** (-0.5)

    def line(which, carry):
        rows = pl.ds(pl.multiple_of(which * length, length), length)
        for pair in range(HEADS // 2):
            lanes = slice(pair * wide, (pair + 1) * wide)
            q, k, v = q_ref[rows, lanes], k_ref[rows, lanes], v_ref[rows, lanes]
            k2, v2 = halves(k, first), halves(v, first)
            scores = dot(q, k2, 1, 1) * scale
            probs = []
            for part in (scores[:, :length], scores[:, length:]):
                e = jnp.exp(part - jnp.max(part, axis=-1, keepdims=True))
                probs.append(e * (1.0 / jnp.sum(e, axis=-1, keepdims=True)))
            low = jnp.concatenate([x.astype(BF) for x in probs], axis=1)
            if a_ref is not None:
                a_ref[rows, lanes] = (dot(low, v2) * gain_ref[:, lanes]).astype(BF)
            if da_ref is not None:
                da = da_ref[rows, lanes]
                dp = dot(da, v2, 1, 1)
                ds = []
                for x, y in zip(probs, (dp[:, :length], dp[:, length:])):
                    xy = x * y
                    mean = jnp.sum(xy, axis=-1, keepdims=True)
                    ds.append(((xy - x * mean) * scale).astype(BF))
                ds = jnp.concatenate(ds, axis=1)
                dq_ref[rows, lanes] = dot(ds, k2).astype(BF)
                dk = dot(ds, q, 0, 0)
                dk_ref[rows, lanes] = jnp.where(first, dk[:length], dk[length:]).astype(BF)
                dv = dot(low, da, 0, 0)
                dv_ref[rows, lanes] = jnp.where(first, dv[:length], dv[length:]).astype(BF)
        return carry

    lax.fori_loop(0, lines, line, 0)


def input_grad(g, u, dq_ref, dk_ref, dv_ref, w_ref):
    dn = dot(dq_ref[...], w_ref[0], 1, 1) + dot(dk_ref[...], w_ref[1], 1, 1)
    dn = dn + dot(dv_ref[...], w_ref[2], 1, 1)
    uf = u.astype(F32)
    r = inverse_rms(uf)
    mean = jnp.mean(dn * uf, axis=-1, keepdims=True)
    return (g.astype(F32) + r * (dn - uf * (r * r * mean))).astype(BF)


def weight_grads(dw_ref, n_ref, a_ref, g_ref, dq_ref, dk_ref, dv_ref):
    for i, (left, right) in enumerate(
        ((n_ref, dq_ref), (n_ref, dk_ref), (n_ref, dv_ref), (a_ref, g_ref))
    ):
        dw_ref[i] = dot(left[...], right[...], 0, 0).astype(dw_ref.dtype)


def row_forward(cfg, x_ref, w_ref, gain_ref, mid_ref, u_ref, n_ref, q_ref, k_ref, v_ref, a_ref):
    nr, nc, ri, cj = cfg
    ct = nr * cj
    u_ref[...] = reorder(x_ref[...], (nc, ri, ct), (1, 0, 2))
    uf = u_ref[...].astype(F32)
    n_ref[...] = (uf * inverse_rms(uf)).astype(BF)
    for i, ref in enumerate((q_ref, k_ref, v_ref)):
        ref[...] = dot(n_ref[...], w_ref[i]).astype(BF)
    attention(ri, q_ref, k_ref, v_ref, a_ref, None, None, None, None, gain_ref)
    mid = (u_ref[...].astype(F32) + dot(a_ref[...], w_ref[3])).astype(BF)
    mid_ref[...] = reorder(mid, (ri, nc, nr, cj), (2, 1, 3, 0))


def column(cfg, x_ref, c_ref, w_ref, gain_ref, out_ref, dmid_ref, dw_ref,
           u_ref, g_ref, n_ref, q_ref, k_ref, v_ref, a_ref, da_ref, dq_ref, dk_ref, dv_ref):
    nr, nc, ri, cj = cfg
    rt = nc * ri
    g_ref[...] = reorder(c_ref[...], (nr, cj, rt), (1, 0, 2))
    da_ref[...] = (dot(g_ref[...], w_ref[3], 1, 1) * gain_ref[...]).astype(BF)
    u_ref[...] = reorder(x_ref[...], (nr * nc, cj, ri), (1, 0, 2))
    uf = u_ref[...].astype(F32)
    n_ref[...] = (uf * inverse_rms(uf)).astype(BF)
    for i, ref in enumerate((q_ref, k_ref, v_ref)):
        ref[...] = dot(n_ref[...], w_ref[i]).astype(BF)
    attention(cj, q_ref, k_ref, v_ref, a_ref, da_ref, dq_ref, dk_ref, dv_ref, gain_ref)
    dmid = input_grad(g_ref[...], u_ref[...], dq_ref, dk_ref, dv_ref, w_ref)
    dmid_ref[...] = reorder(dmid, (cj, nr * nc, ri), (1, 0, 2))
    out = (u_ref[...].astype(F32) + dot(a_ref[...], w_ref[3])).astype(BF)
    out_ref[...] = reorder(out, (cj, nr, rt), (1, 0, 2))
    weight_grads(dw_ref, n_ref, a_ref, g_ref, dq_ref, dk_ref, dv_ref)


def row_backward(cfg, d_ref, w_ref, gain_ref, u_ref, n_ref, q_ref, k_ref, v_ref, a_ref,
                 gin_ref, dw_ref, g_ref, da_ref, dq_ref, dk_ref, dv_ref):
    nr, nc, ri, cj = cfg
    ct = nr * cj
    g_ref[...] = reorder(d_ref[...], (nr, nc, cj, ri), (3, 1, 0, 2))
    da_ref[...] = (dot(g_ref[...], w_ref[3], 1, 1) * gain_ref[...]).astype(BF)
    attention(ri, q_ref, k_ref, v_ref, None, da_ref, dq_ref, dk_ref, dv_ref, gain_ref)
    gin = input_grad(g_ref[...], u_ref[...], dq_ref, dk_ref, dv_ref, w_ref)
    gin_ref[...] = reorder(gin, (ri, nc, ct), (1, 0, 2))
    weight_grads(dw_ref, n_ref, a_ref, g_ref, dq_ref, dk_ref, dv_ref)


def call(kernel, name, n_in, outs, scratch, flops):
    vmem = pl.BlockSpec(memory_space=pltpu.VMEM)
    return pl.pallas_call(
        kernel,
        name=name,
        out_shape=outs,
        in_specs=[vmem] * n_in,
        out_specs=[vmem] * len(outs),
        scratch_shapes=scratch,
        compiler_params=pltpu.CompilerParams(vmem_limit_bytes=40 * 2**20),
        cost_estimate=pl.CostEstimate(flops=flops, bytes_accessed=6 * 2**20, transcendentals=0),
    )


def body(sizes, latents, cotangent, w_row, w_col, keep_heads):
    nr, nc = sizes
    rt, ct, width = latents.shape
    ri, cj = rt // nc, ct // nr
    cfg = (nr, nc, ri, cj)
    tokens = rt * ct
    flat = (tokens, width)
    gains = jnp.repeat(keep_heads.astype(F32), HEAD, axis=1)
    gain_row, gain_col = gains[:1], gains[1:]
    act = jax.ShapeDtypeStruct(flat, BF)
    dw = jax.ShapeDtypeStruct(w_row.shape, BF)
    tile = pltpu.VMEM(flat, BF)
    unit = 2 * tokens * width * width

    def exchange(values, axes, parts):
        pieces = values.reshape(parts, tokens // parts, width)
        return lax.all_to_all(pieces, axes, split_axis=0, concat_axis=0, tiled=True).reshape(flat)

    x_rows = exchange(latents, "col", nc)
    g_cols = exchange(cotangent.transpose(1, 0, 2), "row", nr)
    mid, *saved = call(
        functools.partial(row_forward, cfg), "row_forward", 3, [act] * 7, [], 6 * unit
    )(x_rows, w_row, gain_row)
    x_cols = exchange(mid, ("row", "col"), nr * nc)
    out, dmid, dw_col = call(
        functools.partial(column, cfg), "column", 4, [act, act, dw], [tile] * 11, 16 * unit
    )(x_cols, g_cols, w_col, gain_col)
    g_rows = exchange(dmid, ("row", "col"), nr * nc)
    grad_col = lax.psum(dw_col, ("row", "col")).astype(F32)
    output = exchange(out, "row", nr).reshape(ct, rt, width).transpose(1, 0, 2)
    gin, dw_row = call(
        functools.partial(row_backward, cfg), "row_backward", 9, [act, dw], [tile] * 5, 12 * unit
    )(g_rows, w_row, gain_row, *saved)
    dw_row, grad_col = lax.optimization_barrier((dw_row, grad_col))
    grad_row = lax.psum(dw_row, ("row", "col")).astype(F32)
    grad_latents = exchange(gin, "col", nc).reshape(latents.shape)
    return (output, grad_latents, grad_row, grad_col)


def solution(mesh):
    in_specs = (P("row", "col", None), P("row", "col", None), P(), P(), P())
    out_specs = (P("row", "col", None), P("row", "col", None), P(), P())
    sizes = (mesh.shape["row"], mesh.shape["col"])
    return jax.shard_map(
        functools.partial(body, sizes), mesh=mesh, in_specs=in_specs, out_specs=out_specs,
        check_vma=False,
    )
```

```python
import functools

import jax
import jax.numpy as jnp
from jax import lax
from jax.experimental import pallas as pl
from jax.experimental.pallas import tpu as pltpu
from jax.sharding import PartitionSpec as P

HEADS = 8
HEAD = 64
EPSILON = 1e-06
BF = jnp.bfloat16
F32 = jnp.float32


def dot(left, right, ca=1, cb=0):
    return lax.dot_general(
        left, right, (((ca,), (cb,)), ((), ())), preferred_element_type=F32
    )


def reorder(rows, sizes, order):
    total = rows.shape[0]
    index = lax.broadcasted_iota(jnp.int32, (total, 1), 0)
    strides, stride = [0] * len(sizes), 1
    for axis in reversed(range(len(sizes))):
        strides[axis], stride = stride, stride * sizes[axis]
    source, stride = jnp.zeros_like(index), 1
    for axis in reversed(order):
        digit = lax.rem(lax.div(index, jnp.int32(stride)), jnp.int32(sizes[axis]))
        source = source + digit * strides[axis]
        stride *= sizes[axis]
    column = lax.broadcasted_iota(jnp.int32, (total, total), 1)
    matrix = jnp.where(column == source, 1.0, 0.0).astype(BF)
    return dot(matrix, rows).astype(BF)


def inverse_rms(values):
    return lax.rsqrt(jnp.mean(values * values, axis=-1, keepdims=True) + EPSILON)


def halves(pair, first):
    zero = jnp.zeros_like(pair)
    return jnp.concatenate([jnp.where(first, pair, zero), jnp.where(first, zero, pair)], axis=0)


def attention(lines, q_ref, k_ref, v_ref, a_ref, da_ref, dq_ref, dk_ref, dv_ref, gain_ref):
    length = q_ref.shape[0] // lines
    wide = 2 * HEAD
    first = lax.broadcasted_iota(jnp.int32, (length, wide), 1) < HEAD
    scale = HEAD ** (-0.5)

    def line(which, carry):
        rows = pl.ds(pl.multiple_of(which * length, length), length)
        for pair in range(HEADS // 2):
            lanes = slice(pair * wide, (pair + 1) * wide)
            q, k, v = q_ref[rows, lanes], k_ref[rows, lanes], v_ref[rows, lanes]
            k2, v2 = halves(k, first), halves(v, first)
            scores = dot(q, k2, 1, 1) * scale
            probs = []
            for part in (scores[:, :length], scores[:, length:]):
                e = jnp.exp(part - jnp.max(part, axis=-1, keepdims=True))
                probs.append(e * (1.0 / jnp.sum(e, axis=-1, keepdims=True)))
            low = jnp.concatenate([x.astype(BF) for x in probs], axis=1)
            if a_ref is not None:
                a_ref[rows, lanes] = (dot(low, v2) * gain_ref[:, lanes]).astype(BF)
            if da_ref is not None:
                da = da_ref[rows, lanes]
                dp = dot(da, v2, 1, 1)
                ds = []
                for x, y in zip(probs, (dp[:, :length], dp[:, length:])):
                    xy = x * y
                    mean = jnp.sum(xy, axis=-1, keepdims=True)
                    ds.append(((xy - x * mean) * scale).astype(BF))
                ds = jnp.concatenate(ds, axis=1)
                dq_ref[rows, lanes] = dot(ds, k2).astype(BF)
                dk = dot(ds, q, 0, 0)
                dk_ref[rows, lanes] = jnp.where(first, dk[:length], dk[length:]).astype(BF)
                dv = dot(low, da, 0, 0)
                dv_ref[rows, lanes] = jnp.where(first, dv[:length], dv[length:]).astype(BF)
        return carry

    lax.fori_loop(0, lines, line, 0)


def input_grad(g, u, dq_ref, dk_ref, dv_ref, w_ref):
    dn = dot(dq_ref[...], w_ref[0], 1, 1) + dot(dk_ref[...], w_ref[1], 1, 1)
    dn = dn + dot(dv_ref[...], w_ref[2], 1, 1)
    uf = u.astype(F32)
    r = inverse_rms(uf)
    mean = jnp.mean(dn * uf, axis=-1, keepdims=True)
    return (g.astype(F32) + r * (dn - uf * (r * r * mean))).astype(BF)


def weight_grads(dw_ref, n_ref, a_ref, g_ref, dq_ref, dk_ref, dv_ref):
    for i, (left, right) in enumerate(
        ((n_ref, dq_ref), (n_ref, dk_ref), (n_ref, dv_ref), (a_ref, g_ref))
    ):
        dw_ref[i] = dot(left[...], right[...], 0, 0).astype(dw_ref.dtype)


def row_forward(cfg, x_ref, w_ref, gain_ref, mid_ref, u_ref, n_ref, q_ref, k_ref, v_ref, a_ref):
    nr, nc, ri, cj = cfg
    ct = nr * cj
    u_ref[...] = reorder(x_ref[...], (nc, ri, ct), (1, 0, 2))
    uf = u_ref[...].astype(F32)
    n_ref[...] = (uf * inverse_rms(uf)).astype(BF)
    for i, ref in enumerate((q_ref, k_ref, v_ref)):
        ref[...] = dot(n_ref[...], w_ref[i]).astype(BF)
    attention(ri, q_ref, k_ref, v_ref, a_ref, None, None, None, None, gain_ref)
    mid = (u_ref[...].astype(F32) + dot(a_ref[...], w_ref[3])).astype(BF)
    mid_ref[...] = reorder(mid, (ri, nc, nr, cj), (2, 1, 3, 0))


def column(cfg, x_ref, c_ref, w_ref, gain_ref, out_ref, dmid_ref, dw_ref,
           u_ref, g_ref, n_ref, q_ref, k_ref, v_ref, a_ref, da_ref, dq_ref, dk_ref, dv_ref):
    nr, nc, ri, cj = cfg
    rt = nc * ri
    g_ref[...] = reorder(c_ref[...], (nr, cj, rt), (1, 0, 2))
    da_ref[...] = (dot(g_ref[...], w_ref[3], 1, 1) * gain_ref[...]).astype(BF)
    u_ref[...] = reorder(x_ref[...], (nr * nc, cj, ri), (1, 0, 2))
    uf = u_ref[...].astype(F32)
    n_ref[...] = (uf * inverse_rms(uf)).astype(BF)
    for i, ref in enumerate((q_ref, k_ref, v_ref)):
        ref[...] = dot(n_ref[...], w_ref[i]).astype(BF)
    attention(cj, q_ref, k_ref, v_ref, a_ref, da_ref, dq_ref, dk_ref, dv_ref, gain_ref)
    dmid = input_grad(g_ref[...], u_ref[...], dq_ref, dk_ref, dv_ref, w_ref)
    dmid_ref[...] = reorder(dmid, (cj, nr * nc, ri), (1, 0, 2))
    out = (u_ref[...].astype(F32) + dot(a_ref[...], w_ref[3])).astype(BF)
    out_ref[...] = reorder(out, (cj, nr, rt), (1, 0, 2))
    weight_grads(dw_ref, n_ref, a_ref, g_ref, dq_ref, dk_ref, dv_ref)


def row_backward(cfg, d_ref, w_ref, gain_ref, u_ref, n_ref, q_ref, k_ref, v_ref, a_ref,
                 gin_ref, dw_ref, g_ref, da_ref, dq_ref, dk_ref, dv_ref):
    nr, nc, ri, cj = cfg
    ct = nr * cj
    g_ref[...] = reorder(d_ref[...], (nr, nc, cj, ri), (3, 1, 0, 2))
    da_ref[...] = (dot(g_ref[...], w_ref[3], 1, 1) * gain_ref[...]).astype(BF)
    attention(ri, q_ref, k_ref, v_ref, None, da_ref, dq_ref, dk_ref, dv_ref, gain_ref)
    gin = input_grad(g_ref[...], u_ref[...], dq_ref, dk_ref, dv_ref, w_ref)
    gin_ref[...] = reorder(gin, (ri, nc, ct), (1, 0, 2))
    weight_grads(dw_ref, n_ref, a_ref, g_ref, dq_ref, dk_ref, dv_ref)


def sum_kernel(nr, nc, parts, col_ref, row_ref, out_ref, land0, work0, land1, work1, land2,
               send_sem, recv_sem):
    r, c = lax.axis_index("row"), lax.axis_index("col")
    nz = nc // 2
    z, core = c // 2, lax.rem(c, 2)
    rows = out_ref.shape[0] // parts
    half = rows // 2
    rc = half // nr
    zc = rc // nz
    pair = (r, z * 2 + (1 - core))
    row_peer = [(lax.rem(r + d, nr), c) for d in range(1, nr)]
    z_peer = [(r, lax.rem(z + d, nz) * 2 + core) for d in range(1, nz)]
    peers = [pair] + row_peer + z_peer

    barrier = pltpu.get_barrier_semaphore()
    for peer in peers:
        pl.semaphore_signal(barrier, inc=1, device_id=peer, device_id_type=pl.DeviceIdType.MESH)
    pl.semaphore_wait(barrier, len(peers))

    def span(start, size):
        return pl.ds(pl.multiple_of(start, 16), size)

    def copy(part, slot, source, target, peer):
        made = pltpu.make_async_remote_copy(
            src_ref=source, dst_ref=target, send_sem=send_sem.at[part, slot],
            recv_sem=recv_sem.at[part, slot], device_id=peer,
            device_id_type=pl.DeviceIdType.MESH,
        )
        made.start()
        return made

    def add(size, sources, store):
        step = min(size, 64)
        while size % step:
            step -= 16

        def one(i, carry):
            at = i * step
            total = sources[0](at, step).astype(F32)
            for source in sources[1:]:
                total = total + source(at, step).astype(F32)
            store(at, step, total.astype(BF))
            return carry

        lax.fori_loop(0, size // step, one, 0)

    def reader(ref, base, *lead):
        return lambda at, step: ref[(*lead, span(base + at, step), slice(None))]

    def writer(ref, base, *lead):
        def store(at, step, value):
            ref[(*lead, span(base + at, step), slice(None))] = value

        return store

    def run(part):
        own, local = (col_ref, part) if part < parts // 2 else (row_ref, part - parts // 2)
        start = local * rows
        other = [copy(part, 0, own.at[span(start + (1 - core) * half, half)], land0.at[part], pair)]
        yield other
        add(half, [reader(own, start + core * half), reader(land0, 0, part)],
            writer(work0, 0, part))
        slot = 1
        made = []
        for d, peer in enumerate(row_peer):
            made.append(copy(part, slot, work0.at[part, span(peer[0] * rc, rc)],
                             land1.at[part, d], peer))
            slot += 1
        yield made
        add(rc, [reader(work0, r * rc, part)] + [reader(land1, 0, part, d) for d in range(nr - 1)],
            writer(work1, 0, part))
        made = []
        for d, peer in enumerate(z_peer):
            to = lax.rem(z + d + 1, nz)
            made.append(copy(part, slot, work1.at[part, span(to * zc, zc)],
                             land2.at[part, d], peer))
            slot += 1
        yield made
        base0 = part * rows + core * half
        base1 = base0 + r * rc
        base2 = base1 + z * zc
        add(zc, [reader(work1, z * zc, part)] + [reader(land2, 0, part, d) for d in range(nz - 1)],
            writer(out_ref, base2))
        for base, size, group in ((base2, zc, z_peer), (base1, rc, row_peer), (base0, half, [pair])):
            made = []
            for peer in group:
                block = out_ref.at[span(base, size)]
                made.append(copy(part, slot, block, block, peer))
                slot += 1
            yield made

    runs = [run(part) for part in range(parts)]
    flying = [next(x) for x in runs]
    for stage in range(6):
        for i, x in enumerate(runs):
            for made in flying[i]:
                made.wait()
            flying[i] = next(x, [])


def all_sum(sizes, dw_col, dw_row):
    nr, nc = sizes
    shape, width = dw_col.shape, dw_col.shape[2]
    rows = 2 * shape[0] * shape[1]
    parts = 4 if rows % (4 * nr * nc * 16) == 0 else 2
    half = rows // parts // 2
    rc = half // nr
    nz = nc // 2
    zc = rc // nz
    vmem = pl.BlockSpec(memory_space=pltpu.VMEM)
    slots = 2 * (1 + nr - 1 + nz - 1)
    total = pl.pallas_call(
        functools.partial(sum_kernel, nr, nc, parts),
        name="all_sum",
        out_shape=jax.ShapeDtypeStruct((rows, width), BF),
        in_specs=[vmem, vmem],
        out_specs=vmem,
        scratch_shapes=[
            pltpu.VMEM((parts, half, width), BF),
            pltpu.VMEM((parts, half, width), BF),
            pltpu.VMEM((parts, nr - 1, rc, width), BF),
            pltpu.VMEM((parts, rc, width), BF),
            pltpu.VMEM((parts, nz - 1, zc, width), BF),
            pltpu.SemaphoreType.DMA((parts, slots)),
            pltpu.SemaphoreType.DMA((parts, slots)),
        ],
        compiler_params=pltpu.CompilerParams(
            collective_id=0, has_side_effects=True, vmem_limit_bytes=40 * 2**20
        ),
        cost_estimate=pl.CostEstimate(flops=10**9, bytes_accessed=200 * 2**20, transcendentals=0),
    )(dw_col.reshape(-1, width), dw_row.reshape(-1, width))
    total = total.reshape((2,) + shape)
    return total[1].astype(F32), total[0].astype(F32)


def call(kernel, name, n_in, outs, scratch, flops):
    vmem = pl.BlockSpec(memory_space=pltpu.VMEM)
    return pl.pallas_call(
        kernel,
        name=name,
        out_shape=outs,
        in_specs=[vmem] * n_in,
        out_specs=[vmem] * len(outs),
        scratch_shapes=scratch,
        compiler_params=pltpu.CompilerParams(vmem_limit_bytes=40 * 2**20),
        cost_estimate=pl.CostEstimate(flops=flops, bytes_accessed=6 * 2**20, transcendentals=0),
    )


def body(sizes, latents, cotangent, w_row, w_col, keep_heads):
    nr, nc = sizes
    rt, ct, width = latents.shape
    ri, cj = rt // nc, ct // nr
    cfg = (nr, nc, ri, cj)
    tokens = rt * ct
    flat = (tokens, width)
    gains = jnp.repeat(keep_heads.astype(F32), HEAD, axis=1)
    gain_row, gain_col = gains[:1], gains[1:]
    act = jax.ShapeDtypeStruct(flat, BF)
    dw = jax.ShapeDtypeStruct(w_row.shape, BF)
    tile = pltpu.VMEM(flat, BF)
    unit = 2 * tokens * width * width

    def exchange(values, axes, parts):
        pieces = values.reshape(parts, tokens // parts, width)
        return lax.all_to_all(pieces, axes, split_axis=0, concat_axis=0, tiled=True).reshape(flat)

    x_rows = exchange(latents, "col", nc)
    g_cols = exchange(cotangent.transpose(1, 0, 2), "row", nr)
    mid, *saved = call(
        functools.partial(row_forward, cfg), "row_forward", 3, [act] * 7, [], 6 * unit
    )(x_rows, w_row, gain_row)
    x_cols = exchange(mid, ("row", "col"), nr * nc)
    out, dmid, dw_col = call(
        functools.partial(column, cfg), "column", 4, [act, act, dw], [tile] * 11, 16 * unit
    )(x_cols, g_cols, w_col, gain_col)
    g_rows = exchange(dmid, ("row", "col"), nr * nc)
    output = exchange(out, "row", nr).reshape(ct, rt, width).transpose(1, 0, 2)
    gin, dw_row = call(
        functools.partial(row_backward, cfg), "row_backward", 9, [act, dw], [tile] * 5, 12 * unit
    )(g_rows, w_row, gain_row, *saved)
    grad_latents = exchange(gin, "col", nc).reshape(latents.shape)
    grad_row, grad_col = all_sum(sizes, dw_col, dw_row)
    return (output, grad_latents, grad_row, grad_col)


def solution(mesh):
    in_specs = (P("row", "col", None), P("row", "col", None), P(), P(), P())
    out_specs = (P("row", "col", None), P("row", "col", None), P(), P())
    sizes = (mesh.shape["row"], mesh.shape["col"])
    return jax.shard_map(
        functools.partial(body, sizes), mesh=mesh, in_specs=in_specs, out_specs=out_specs,
        check_vma=False,
    )
```

```python
import functools

import jax
import jax.numpy as jnp
from jax import lax
from jax.experimental import pallas as pl
from jax.experimental.pallas import tpu as pltpu
from jax.sharding import PartitionSpec as P

HEADS = 8
HEAD = 64
EPSILON = 1e-06
BF = jnp.bfloat16
F32 = jnp.float32


def dot(left, right, ca=1, cb=0):
    return lax.dot_general(
        left, right, (((ca,), (cb,)), ((), ())), preferred_element_type=F32
    )


def reorder(rows, sizes, order):
    total = rows.shape[0]
    index = lax.broadcasted_iota(jnp.int32, (total, 1), 0)
    strides, stride = [0] * len(sizes), 1
    for axis in reversed(range(len(sizes))):
        strides[axis], stride = stride, stride * sizes[axis]
    source, stride = jnp.zeros_like(index), 1
    for axis in reversed(order):
        digit = lax.rem(lax.div(index, jnp.int32(stride)), jnp.int32(sizes[axis]))
        source = source + digit * strides[axis]
        stride *= sizes[axis]
    column = lax.broadcasted_iota(jnp.int32, (total, total), 1)
    matrix = jnp.where(column == source, 1.0, 0.0).astype(BF)
    return dot(matrix, rows).astype(BF)


def inverse_rms(values):
    return lax.rsqrt(jnp.mean(values * values, axis=-1, keepdims=True) + EPSILON)


def halves(pair, first):
    zero = jnp.zeros_like(pair)
    return jnp.concatenate([jnp.where(first, pair, zero), jnp.where(first, zero, pair)], axis=0)


def attention(lines, q_ref, k_ref, v_ref, a_ref, da_ref, dq_ref, dk_ref, dv_ref, gain_ref):
    length = q_ref.shape[0] // lines
    wide = 2 * HEAD
    first = lax.broadcasted_iota(jnp.int32, (length, wide), 1) < HEAD
    scale = HEAD ** (-0.5)

    def line(which, carry):
        rows = pl.ds(pl.multiple_of(which * length, length), length)
        for pair in range(HEADS // 2):
            lanes = slice(pair * wide, (pair + 1) * wide)
            q, k, v = q_ref[rows, lanes], k_ref[rows, lanes], v_ref[rows, lanes]
            k2, v2 = halves(k, first), halves(v, first)
            scores = dot(q, k2, 1, 1) * scale
            probs = []
            for part in (scores[:, :length], scores[:, length:]):
                e = jnp.exp(part - jnp.max(part, axis=-1, keepdims=True))
                probs.append(e * (1.0 / jnp.sum(e, axis=-1, keepdims=True)))
            low = jnp.concatenate([x.astype(BF) for x in probs], axis=1)
            if a_ref is not None:
                a_ref[rows, lanes] = (dot(low, v2) * gain_ref[:, lanes]).astype(BF)
            if da_ref is not None:
                da = da_ref[rows, lanes]
                dp = dot(da, v2, 1, 1)
                ds = []
                for x, y in zip(probs, (dp[:, :length], dp[:, length:])):
                    xy = x * y
                    mean = jnp.sum(xy, axis=-1, keepdims=True)
                    ds.append(((xy - x * mean) * scale).astype(BF))
                ds = jnp.concatenate(ds, axis=1)
                dq_ref[rows, lanes] = dot(ds, k2).astype(BF)
                dk = dot(ds, q, 0, 0)
                dk_ref[rows, lanes] = jnp.where(first, dk[:length], dk[length:]).astype(BF)
                dv = dot(low, da, 0, 0)
                dv_ref[rows, lanes] = jnp.where(first, dv[:length], dv[length:]).astype(BF)
        return carry

    lax.fori_loop(0, lines, line, 0)


def input_grad(g, u, dq_ref, dk_ref, dv_ref, w_ref):
    dn = dot(dq_ref[...], w_ref[0], 1, 1) + dot(dk_ref[...], w_ref[1], 1, 1)
    dn = dn + dot(dv_ref[...], w_ref[2], 1, 1)
    uf = u.astype(F32)
    r = inverse_rms(uf)
    mean = jnp.mean(dn * uf, axis=-1, keepdims=True)
    return (g.astype(F32) + r * (dn - uf * (r * r * mean))).astype(BF)


def weight_grads(dw_ref, n_ref, a_ref, g_ref, dq_ref, dk_ref, dv_ref):
    for i, (left, right) in enumerate(
        ((n_ref, dq_ref), (n_ref, dk_ref), (n_ref, dv_ref), (a_ref, g_ref))
    ):
        width = left.shape[1]
        dw_ref[i * width:(i + 1) * width, :] = dot(left[...], right[...], 0, 0).astype(BF)


def row_forward(cfg, x_ref, w_ref, gain_ref, mid_ref, u_ref, a_ref, n_ref, q_ref, k_ref, v_ref):
    nr, nc, ri, cj = cfg
    ct = nr * cj
    u_ref[...] = reorder(x_ref[...], (nc, ri, ct), (1, 0, 2))
    uf = u_ref[...].astype(F32)
    n_ref[...] = (uf * inverse_rms(uf)).astype(BF)
    for i, ref in enumerate((q_ref, k_ref, v_ref)):
        ref[...] = dot(n_ref[...], w_ref[i]).astype(BF)
    attention(ri, q_ref, k_ref, v_ref, a_ref, None, None, None, None, gain_ref)
    mid = (u_ref[...].astype(F32) + dot(a_ref[...], w_ref[3])).astype(BF)
    mid_ref[...] = reorder(mid, (ri, nc, nr, cj), (2, 1, 3, 0))


def column(cfg, x_ref, c_ref, w_ref, gain_ref, out_ref, dmid_ref, dw_ref,
           u_ref, g_ref, n_ref, q_ref, k_ref, v_ref, a_ref, da_ref, dq_ref, dk_ref, dv_ref):
    nr, nc, ri, cj = cfg
    rt = nc * ri
    g_ref[...] = reorder(c_ref[...], (nr, cj, rt), (1, 0, 2))
    da_ref[...] = (dot(g_ref[...], w_ref[3], 1, 1) * gain_ref[...]).astype(BF)
    u_ref[...] = reorder(x_ref[...], (nr * nc, cj, ri), (1, 0, 2))
    uf = u_ref[...].astype(F32)
    n_ref[...] = (uf * inverse_rms(uf)).astype(BF)
    for i, ref in enumerate((q_ref, k_ref, v_ref)):
        ref[...] = dot(n_ref[...], w_ref[i]).astype(BF)
    attention(cj, q_ref, k_ref, v_ref, a_ref, da_ref, dq_ref, dk_ref, dv_ref, gain_ref)
    dmid = input_grad(g_ref[...], u_ref[...], dq_ref, dk_ref, dv_ref, w_ref)
    dmid_ref[...] = reorder(dmid, (cj, nr * nc, ri), (1, 0, 2))
    out = (u_ref[...].astype(F32) + dot(a_ref[...], w_ref[3])).astype(BF)
    out_ref[...] = reorder(out, (cj, nr, rt), (1, 0, 2))
    weight_grads(dw_ref, n_ref, a_ref, g_ref, dq_ref, dk_ref, dv_ref)


def finish(cfg, parts, d_ref, col_ref, w_ref, gain_ref, u_ref, a_ref, out_ref, glat_ref, row_ref, n_ref, q_ref, k_ref, v_ref,
            hop1, turned, hop2, gin_ref, g_ref, da_ref, dq_ref, dk_ref,
           dv_ref, land0, work0, land1, work1, land2, send_sem, recv_sem, hop1_sem, hop2_sem,
           gin_sem):
    nr, nc, ri, cj = cfg
    tokens = d_ref.shape[0]
    r, c = lax.axis_index("row"), lax.axis_index("col")
    nz = nc // 2
    z, core = c // 2, lax.rem(c, 2)
    rows = out_ref.shape[0] // parts
    half = rows // 2
    rc = half // nr
    zc = rc // nz
    pair = (r, z * 2 + (1 - core))
    row_peer = [(lax.rem(r + d, nr), c) for d in range(1, nr)]
    col_peer = [(r, lax.rem(c + d, nc)) for d in range(1, nc)]
    z_peer = [(r, lax.rem(z + d, nz) * 2 + core) for d in range(1, nz)]
    peers = row_peer + col_peer

    barrier = pltpu.get_barrier_semaphore()
    for peer in peers:
        pl.semaphore_signal(barrier, inc=1, device_id=peer, device_id_type=pl.DeviceIdType.MESH)
    pl.semaphore_wait(barrier, len(peers))

    def span(start, size):
        return pl.ds(pl.multiple_of(start, 16), size)

    def copy(part, slot, source, target, peer):
        made = pltpu.make_async_remote_copy(
            src_ref=source, dst_ref=target, send_sem=send_sem.at[part, slot],
            recv_sem=recv_sem.at[part, slot], device_id=peer,
            device_id_type=pl.DeviceIdType.MESH,
        )
        made.start()
        return made

    def add(size, sources, store):
        step = min(size, 64)
        while size % step:
            step -= 16

        def one(i, carry):
            at = i * step
            total = sources[0](at, step).astype(F32)
            for source in sources[1:]:
                total = total + source(at, step).astype(F32)
            store(at, step, total.astype(BF))
            return carry

        lax.fori_loop(0, size // step, one, 0)

    def reader(ref, base, *lead):
        return lambda at, step: ref[(*lead, span(base + at, step), slice(None))]

    def writer(ref, base, *lead):
        def store(at, step, value):
            ref[(*lead, span(base + at, step), slice(None))] = value

        return store

    def run(part):
        own, local = (col_ref, part) if part < parts // 2 else (row_ref, part - parts // 2)
        start = local * rows
        other = [copy(part, 0, own.at[span(start + (1 - core) * half, half)], land0.at[part], pair)]
        yield other
        add(half, [reader(own, start + core * half), reader(land0, 0, part)],
            writer(work0, 0, part))
        slot = 1
        made = []
        for d, peer in enumerate(row_peer):
            made.append(copy(part, slot, work0.at[part, span(peer[0] * rc, rc)],
                             land1.at[part, d], peer))
            slot += 1
        yield made
        add(rc, [reader(work0, r * rc, part)] + [reader(land1, 0, part, d) for d in range(nr - 1)],
            writer(work1, 0, part))
        made = []
        for d, peer in enumerate(z_peer):
            to = lax.rem(z + d + 1, nz)
            made.append(copy(part, slot, work1.at[part, span(to * zc, zc)],
                             land2.at[part, d], peer))
            slot += 1
        yield made
        base0 = part * rows + core * half
        base1 = base0 + r * rc
        base2 = base1 + z * zc
        add(zc, [reader(work1, z * zc, part)] + [reader(land2, 0, part, d) for d in range(nz - 1)],
            writer(out_ref, base2))
        for base, size, group in ((base2, zc, z_peer), (base1, rc, row_peer), (base0, half, [pair])):
            made = []
            for peer in group:
                block = out_ref.at[span(base, size)]
                made.append(copy(part, slot, block, block, peer))
                slot += 1
            yield made

    def exchange(source, target, size, mine, group, axis, sems):
        made = []
        for d, peer in enumerate(group):
            copied = pltpu.make_async_remote_copy(
                src_ref=source.at[span(peer[axis] * size, size)],
                dst_ref=target.at[span(mine * size, size)],
                send_sem=sems.at[0, d], recv_sem=sems.at[1, d], device_id=peer,
                device_id_type=pl.DeviceIdType.MESH,
            )
            copied.start()
            made.append(copied)
        target[span(mine * size, size), :] = source[span(mine * size, size), :]
        return made

    def finished(made):
        for copied in made:
            copied.wait()

    flying = {}

    def begin(part):
        steps = run(part)
        flying[part] = (steps, next(steps))

    def advance(which):
        for part in which:
            steps, made = flying[part]
            finished(made)
            flying[part] = (steps, next(steps, []))

    cols, later = range(parts // 2), range(parts // 2, parts)
    made = exchange(d_ref, hop1, tokens // nr, r, row_peer, 0, hop1_sem)
    for part in cols:
        begin(part)
    uf = u_ref[...].astype(F32)
    n_ref[...] = (uf * inverse_rms(uf)).astype(BF)
    for i, ref in enumerate((q_ref, k_ref, v_ref)):
        ref[...] = dot(n_ref[...], w_ref[i]).astype(BF)
    finished(made)
    turned[...] = reorder(hop1[...], (nr, nc, cj * ri), (1, 0, 2))
    made = exchange(turned, hop2, tokens // nc, c, col_peer, 1, hop2_sem)
    advance(cols)
    finished(made)
    g_ref[...] = reorder(hop2[...], (nc, nr, cj, ri), (3, 0, 1, 2))
    da_ref[...] = (dot(g_ref[...], w_ref[3], 1, 1) * gain_ref[...]).astype(BF)
    advance(cols)
    attention(ri, q_ref, k_ref, v_ref, None, da_ref, dq_ref, dk_ref, dv_ref, gain_ref)
    weight_grads(row_ref, n_ref, a_ref, g_ref, dq_ref, dk_ref, dv_ref)
    advance(cols)
    for part in later:
        begin(part)
    gin = input_grad(g_ref[...], u_ref[...], dq_ref, dk_ref, dv_ref, w_ref)
    gin_ref[...] = reorder(gin, (ri, nc, nr * cj), (1, 0, 2))
    advance(later)
    advance(cols)
    made = exchange(gin_ref, glat_ref, tokens // nc, c, col_peer, 1, gin_sem)
    advance(later)
    advance(cols)
    advance(later)
    advance(cols)
    for _ in range(3):
        advance(later)
    finished(made)


def last_kernel(cfg, dmid, dw_col, w_row, gain_row, saved):
    nr, nc = cfg[:2]
    shape, width = w_row.shape, w_row.shape[2]
    rows = 2 * shape[0] * shape[1]
    parts = 4 if rows % (4 * nr * nc * 16) == 0 else 2
    half = rows // parts // 2
    rc = half // nr
    nz = nc // 2
    zc = rc // nz
    vmem = pl.BlockSpec(memory_space=pltpu.VMEM)
    slots = 2 * (1 + nr - 1 + nz - 1)
    tile = pltpu.VMEM(dmid.shape, BF)
    total, glat = pl.pallas_call(
        functools.partial(finish, cfg, parts),
        name="finish",
        out_shape=[jax.ShapeDtypeStruct((rows, width), BF), jax.ShapeDtypeStruct(dmid.shape, BF)],
        in_specs=[vmem] * 6,
        out_specs=[vmem] * 2,
        scratch_shapes=[
            pltpu.VMEM((rows // 2, width), BF),
        ] + [tile] * 13 + [
            pltpu.VMEM((parts, half, width), BF),
            pltpu.VMEM((parts, half, width), BF),
            pltpu.VMEM((parts, nr - 1, rc, width), BF),
            pltpu.VMEM((parts, rc, width), BF),
            pltpu.VMEM((parts, nz - 1, zc, width), BF),
            pltpu.SemaphoreType.DMA((parts, slots)),
            pltpu.SemaphoreType.DMA((parts, slots)),
            pltpu.SemaphoreType.DMA((2, nr - 1)),
            pltpu.SemaphoreType.DMA((2, nc - 1)),
            pltpu.SemaphoreType.DMA((2, nc - 1)),
        ],
        compiler_params=pltpu.CompilerParams(
            collective_id=0, has_side_effects=True, vmem_limit_bytes=36 * 2**20
        ),
        cost_estimate=pl.CostEstimate(flops=10**9, bytes_accessed=200 * 2**20, transcendentals=0),
    )(dmid, dw_col, w_row, gain_row, *saved)
    total = total.reshape((2,) + shape)
    return total[1].astype(F32), total[0].astype(F32), glat


def call(kernel, name, n_in, outs, scratch, flops):
    vmem = pl.BlockSpec(memory_space=pltpu.VMEM)
    return pl.pallas_call(
        kernel,
        name=name,
        out_shape=outs,
        in_specs=[vmem] * n_in,
        out_specs=[vmem] * len(outs),
        scratch_shapes=scratch,
        compiler_params=pltpu.CompilerParams(vmem_limit_bytes=24 * 2**20),
        cost_estimate=pl.CostEstimate(flops=flops, bytes_accessed=6 * 2**20, transcendentals=0),
    )


def body(sizes, latents, cotangent, w_row, w_col, keep_heads):
    nr, nc = sizes
    rt, ct, width = latents.shape
    ri, cj = rt // nc, ct // nr
    cfg = (nr, nc, ri, cj)
    tokens = rt * ct
    flat = (tokens, width)
    gains = jnp.repeat(keep_heads.astype(F32), HEAD, axis=1)
    gain_row, gain_col = gains[:1], gains[1:]
    act = jax.ShapeDtypeStruct(flat, BF)
    dw = jax.ShapeDtypeStruct((w_row.shape[0] * width, width), BF)
    tile = pltpu.VMEM(flat, BF)
    unit = 2 * tokens * width * width

    def exchange(values, axes, parts):
        pieces = values.reshape(parts, tokens // parts, width)
        return lax.all_to_all(pieces, axes, split_axis=0, concat_axis=0, tiled=True).reshape(flat)

    x_rows = exchange(latents, "col", nc)
    g_cols = exchange(cotangent.transpose(1, 0, 2), "row", nr)
    mid, *saved = call(
        functools.partial(row_forward, cfg), "row_forward", 3, [act] * 3, [tile] * 4, 6 * unit
    )(x_rows, w_row, gain_row)
    x_cols = exchange(mid, ("row", "col"), nr * nc)
    out, dmid, dw_col = call(
        functools.partial(column, cfg), "column", 4, [act, act, dw], [tile] * 11, 16 * unit
    )(x_cols, g_cols, w_col, gain_col)
    output = exchange(out, "row", nr).reshape(ct, rt, width).transpose(1, 0, 2)
    grad_row, grad_col, glat = last_kernel(cfg, dmid, dw_col, w_row, gain_row, saved)
    grad_latents = glat.reshape(latents.shape)
    return (output, grad_latents, grad_row, grad_col)


def solution(mesh):
    in_specs = (P("row", "col", None), P("row", "col", None), P(), P(), P())
    out_specs = (P("row", "col", None), P("row", "col", None), P(), P())
    sizes = (mesh.shape["row"], mesh.shape["col"])
    return jax.shard_map(
        functools.partial(body, sizes), mesh=mesh, in_specs=in_specs, out_specs=out_specs,
        check_vma=False,
    )
```

```python
import functools

import jax
import jax.numpy as jnp
from jax import lax
from jax.experimental import pallas as pl
from jax.experimental.pallas import tpu as pltpu
from jax.sharding import PartitionSpec as P

HEADS = 8
HEAD = 64
EPSILON = 1e-06
BF = jnp.bfloat16
F32 = jnp.float32


def dot(left, right, ca=1, cb=0):
    return lax.dot_general(
        left, right, (((ca,), (cb,)), ((), ())), preferred_element_type=F32
    )


def reorder(rows, sizes, order):
    total = rows.shape[0]
    index = lax.broadcasted_iota(jnp.int32, (total, 1), 0)
    strides, stride = [0] * len(sizes), 1
    for axis in reversed(range(len(sizes))):
        strides[axis], stride = stride, stride * sizes[axis]
    source, stride = jnp.zeros_like(index), 1
    for axis in reversed(order):
        digit = lax.rem(lax.div(index, jnp.int32(stride)), jnp.int32(sizes[axis]))
        source = source + digit * strides[axis]
        stride *= sizes[axis]
    column = lax.broadcasted_iota(jnp.int32, (total, total), 1)
    matrix = jnp.where(column == source, 1.0, 0.0).astype(BF)
    return dot(matrix, rows).astype(BF)


def inverse_rms(values):
    return lax.rsqrt(jnp.mean(values * values, axis=-1, keepdims=True) + EPSILON)


def halves(pair, first):
    zero = jnp.zeros_like(pair)
    return jnp.concatenate([jnp.where(first, pair, zero), jnp.where(first, zero, pair)], axis=0)


def attention(lines, q_ref, k_ref, v_ref, a_ref, da_ref, dq_ref, dk_ref, dv_ref, gain_ref):
    length = q_ref.shape[0] // lines
    wide = 2 * HEAD
    first = lax.broadcasted_iota(jnp.int32, (length, wide), 1) < HEAD
    scale = HEAD ** (-0.5)

    def line(which, carry):
        rows = pl.ds(pl.multiple_of(which * length, length), length)
        for pair in range(HEADS // 2):
            lanes = slice(pair * wide, (pair + 1) * wide)
            q, k, v = q_ref[rows, lanes], k_ref[rows, lanes], v_ref[rows, lanes]
            k2, v2 = halves(k, first), halves(v, first)
            scores = dot(q, k2, 1, 1) * scale
            probs = []
            for part in (scores[:, :length], scores[:, length:]):
                e = jnp.exp(part - jnp.max(part, axis=-1, keepdims=True))
                probs.append(e * (1.0 / jnp.sum(e, axis=-1, keepdims=True)))
            low = jnp.concatenate([x.astype(BF) for x in probs], axis=1)
            if a_ref is not None:
                a_ref[rows, lanes] = (dot(low, v2) * gain_ref[:, lanes]).astype(BF)
            if da_ref is not None:
                da = da_ref[rows, lanes]
                dp = dot(da, v2, 1, 1)
                ds = []
                for x, y in zip(probs, (dp[:, :length], dp[:, length:])):
                    xy = x * y
                    mean = jnp.sum(xy, axis=-1, keepdims=True)
                    ds.append(((xy - x * mean) * scale).astype(BF))
                ds = jnp.concatenate(ds, axis=1)
                dq_ref[rows, lanes] = dot(ds, k2).astype(BF)
                dk = dot(ds, q, 0, 0)
                dk_ref[rows, lanes] = jnp.where(first, dk[:length], dk[length:]).astype(BF)
                dv = dot(low, da, 0, 0)
                dv_ref[rows, lanes] = jnp.where(first, dv[:length], dv[length:]).astype(BF)
        return carry

    lax.fori_loop(0, lines, line, 0)


def input_grad(g, u, dq_ref, dk_ref, dv_ref, w_ref):
    dn = dot(dq_ref[...], w_ref[0], 1, 1) + dot(dk_ref[...], w_ref[1], 1, 1)
    dn = dn + dot(dv_ref[...], w_ref[2], 1, 1)
    uf = u.astype(F32)
    r = inverse_rms(uf)
    mean = jnp.mean(dn * uf, axis=-1, keepdims=True)
    return (g.astype(F32) + r * (dn - uf * (r * r * mean))).astype(BF)


def weight_grads(dw_ref, n_ref, a_ref, g_ref, dq_ref, dk_ref, dv_ref):
    for i, (left, right) in enumerate(
        ((n_ref, dq_ref), (n_ref, dk_ref), (n_ref, dv_ref), (a_ref, g_ref))
    ):
        width = left.shape[1]
        dw_ref[i * width:(i + 1) * width, :] = dot(left[...], right[...], 0, 0).astype(BF)


def greet(peers):
    barrier = pltpu.get_barrier_semaphore()
    for peer in peers:
        pl.semaphore_signal(barrier, inc=1, device_id=peer, device_id_type=pl.DeviceIdType.MESH)
    pl.semaphore_wait(barrier, len(peers))


def span(start, size):
    return pl.ds(pl.multiple_of(start, 16), size)


def exchange(source, target, size, mine, group, axis, sems):
    made = []
    for d, peer in enumerate(group):
        copied = pltpu.make_async_remote_copy(
            src_ref=source.at[span(peer[axis] * size, size)],
            dst_ref=target.at[span(mine * size, size)],
            send_sem=sems.at[0, d], recv_sem=sems.at[1, d], device_id=peer,
            device_id_type=pl.DeviceIdType.MESH,
        )
        copied.start()
        made.append(copied)
    target[span(mine * size, size), :] = source[span(mine * size, size), :]
    return made


def finished(made):
    for copied in made:
        copied.wait()


def front(cfg, lat_ref, cot_ref, w_row_ref, gain_row_ref, w_ref, gain_ref,
          ur_ref, ar_ref, out_ref, dmid_ref, dw_ref,
          x_ref, mid_ref, hop1, turned, hop2, send_ref, c_ref, n_ref, q_ref, k_ref, v_ref,
          u_ref, g_ref, a_ref, da_ref, dq_ref, dk_ref, dv_ref, lat_sem, cot_sem, hop1_sem, hop2_sem):
    nr, nc, ri, cj = cfg
    rt, ct = nc * ri, nr * cj
    tokens = lat_ref.shape[0]
    r, c = lax.axis_index("row"), lax.axis_index("col")
    row_peer = [(lax.rem(r + d, nr), c) for d in range(1, nr)]
    col_peer = [(r, lax.rem(c + d, nc)) for d in range(1, nc)]
    greet(row_peer + col_peer)
    lat = exchange(lat_ref, x_ref, tokens // nc, c, col_peer, 1, lat_sem)
    send_ref[...] = reorder(cot_ref[...], (rt, ct), (1, 0))
    cot = exchange(send_ref, c_ref, tokens // nr, r, row_peer, 0, cot_sem)
    finished(lat)
    ur_ref[...] = reorder(x_ref[...], (nc, ri, ct), (1, 0, 2))
    uf = ur_ref[...].astype(F32)
    n_ref[...] = (uf * inverse_rms(uf)).astype(BF)
    for i, ref in enumerate((q_ref, k_ref, v_ref)):
        ref[...] = dot(n_ref[...], w_row_ref[i]).astype(BF)
    attention(ri, q_ref, k_ref, v_ref, ar_ref, None, None, None, None, gain_row_ref)
    mid = (ur_ref[...].astype(F32) + dot(ar_ref[...], w_row_ref[3])).astype(BF)
    mid_ref[...] = reorder(mid, (ri, nc, nr, cj), (1, 2, 3, 0))
    made = exchange(mid_ref, hop1, tokens // nc, c, col_peer, 1, hop1_sem)
    finished(cot)
    g_ref[...] = reorder(c_ref[...], (nr, cj, rt), (1, 0, 2))
    da_ref[...] = (dot(g_ref[...], w_ref[3], 1, 1) * gain_ref[...]).astype(BF)
    finished(made)
    turned[...] = reorder(hop1[...], (nc, nr, cj * ri), (1, 0, 2))
    finished(exchange(turned, hop2, tokens // nr, r, row_peer, 0, hop2_sem))
    u_ref[...] = reorder(hop2[...], (nr * nc, cj, ri), (1, 0, 2))
    uf = u_ref[...].astype(F32)
    n_ref[...] = (uf * inverse_rms(uf)).astype(BF)
    for i, ref in enumerate((q_ref, k_ref, v_ref)):
        ref[...] = dot(n_ref[...], w_ref[i]).astype(BF)
    attention(cj, q_ref, k_ref, v_ref, a_ref, da_ref, dq_ref, dk_ref, dv_ref, gain_ref)
    dmid = input_grad(g_ref[...], u_ref[...], dq_ref, dk_ref, dv_ref, w_ref)
    dmid_ref[...] = reorder(dmid, (cj, nr, nc, ri), (1, 2, 0, 3))
    out = (u_ref[...].astype(F32) + dot(a_ref[...], w_ref[3])).astype(BF)
    out_ref[...] = reorder(out, (cj, nr, rt), (1, 0, 2))
    weight_grads(dw_ref, n_ref, a_ref, g_ref, dq_ref, dk_ref, dv_ref)


def finish(cfg, parts, d_ref, col_ref, w_ref, gain_ref, u_ref, a_ref, out_ref, glat_ref, row_ref, n_ref, q_ref, k_ref, v_ref,
            hop1, turned, hop2, gin_ref, g_ref, da_ref, dq_ref, dk_ref,
           dv_ref, land0, work0, land1, work1, land2, send_sem, recv_sem, hop1_sem, hop2_sem,
           gin_sem):
    nr, nc, ri, cj = cfg
    tokens = d_ref.shape[0]
    r, c = lax.axis_index("row"), lax.axis_index("col")
    nz = nc // 2
    z, core = c // 2, lax.rem(c, 2)
    rows = out_ref.shape[0] // parts
    half = rows // 2
    rc = half // nr
    zc = rc // nz
    pair = (r, z * 2 + (1 - core))
    row_peer = [(lax.rem(r + d, nr), c) for d in range(1, nr)]
    col_peer = [(r, lax.rem(c + d, nc)) for d in range(1, nc)]
    z_peer = [(r, lax.rem(z + d, nz) * 2 + core) for d in range(1, nz)]
    peers = row_peer + col_peer

    greet(peers)

    def copy(part, slot, source, target, peer):
        made = pltpu.make_async_remote_copy(
            src_ref=source, dst_ref=target, send_sem=send_sem.at[part, slot],
            recv_sem=recv_sem.at[part, slot], device_id=peer,
            device_id_type=pl.DeviceIdType.MESH,
        )
        made.start()
        return made

    def add(size, sources, store):
        step = min(size, 64)
        while size % step:
            step -= 16

        def one(i, carry):
            at = i * step
            total = sources[0](at, step).astype(F32)
            for source in sources[1:]:
                total = total + source(at, step).astype(F32)
            store(at, step, total.astype(BF))
            return carry

        lax.fori_loop(0, size // step, one, 0)

    def reader(ref, base, *lead):
        return lambda at, step: ref[(*lead, span(base + at, step), slice(None))]

    def writer(ref, base, *lead):
        def store(at, step, value):
            ref[(*lead, span(base + at, step), slice(None))] = value

        return store

    def run(part):
        own, local = (col_ref, part) if part < parts // 2 else (row_ref, part - parts // 2)
        start = local * rows
        other = [copy(part, 0, own.at[span(start + (1 - core) * half, half)], land0.at[part], pair)]
        yield other
        add(half, [reader(own, start + core * half), reader(land0, 0, part)],
            writer(work0, 0, part))
        slot = 1
        made = []
        for d, peer in enumerate(row_peer):
            made.append(copy(part, slot, work0.at[part, span(peer[0] * rc, rc)],
                             land1.at[part, d], peer))
            slot += 1
        yield made
        add(rc, [reader(work0, r * rc, part)] + [reader(land1, 0, part, d) for d in range(nr - 1)],
            writer(work1, 0, part))
        made = []
        for d, peer in enumerate(z_peer):
            to = lax.rem(z + d + 1, nz)
            made.append(copy(part, slot, work1.at[part, span(to * zc, zc)],
                             land2.at[part, d], peer))
            slot += 1
        yield made
        base0 = part * rows + core * half
        base1 = base0 + r * rc
        base2 = base1 + z * zc
        add(zc, [reader(work1, z * zc, part)] + [reader(land2, 0, part, d) for d in range(nz - 1)],
            writer(out_ref, base2))
        for base, size, group in ((base2, zc, z_peer), (base1, rc, row_peer), (base0, half, [pair])):
            made = []
            for peer in group:
                block = out_ref.at[span(base, size)]
                made.append(copy(part, slot, block, block, peer))
                slot += 1
            yield made

    flying = {}

    def begin(part):
        steps = run(part)
        flying[part] = (steps, next(steps))

    def advance(which):
        for part in which:
            steps, made = flying[part]
            finished(made)
            flying[part] = (steps, next(steps, []))

    cols, later = range(parts // 2), range(parts // 2, parts)
    made = exchange(d_ref, hop1, tokens // nr, r, row_peer, 0, hop1_sem)
    for part in cols:
        begin(part)
    uf = u_ref[...].astype(F32)
    n_ref[...] = (uf * inverse_rms(uf)).astype(BF)
    for i, ref in enumerate((q_ref, k_ref, v_ref)):
        ref[...] = dot(n_ref[...], w_ref[i]).astype(BF)
    finished(made)
    turned[...] = reorder(hop1[...], (nr, nc, cj * ri), (1, 0, 2))
    made = exchange(turned, hop2, tokens // nc, c, col_peer, 1, hop2_sem)
    advance(cols)
    finished(made)
    g_ref[...] = reorder(hop2[...], (nc, nr, cj, ri), (3, 0, 1, 2))
    da_ref[...] = (dot(g_ref[...], w_ref[3], 1, 1) * gain_ref[...]).astype(BF)
    advance(cols)
    attention(ri, q_ref, k_ref, v_ref, None, da_ref, dq_ref, dk_ref, dv_ref, gain_ref)
    weight_grads(row_ref, n_ref, a_ref, g_ref, dq_ref, dk_ref, dv_ref)
    advance(cols)
    for part in later:
        begin(part)
    gin = input_grad(g_ref[...], u_ref[...], dq_ref, dk_ref, dv_ref, w_ref)
    gin_ref[...] = reorder(gin, (ri, nc, nr * cj), (1, 0, 2))
    advance(later)
    advance(cols)
    made = exchange(gin_ref, glat_ref, tokens // nc, c, col_peer, 1, gin_sem)
    advance(later)
    advance(cols)
    advance(later)
    advance(cols)
    for _ in range(3):
        advance(later)
    finished(made)


def last_kernel(cfg, dmid, dw_col, w_row, gain_row, saved):
    nr, nc = cfg[:2]
    shape, width = w_row.shape, w_row.shape[2]
    rows = 2 * shape[0] * shape[1]
    parts = 4 if rows % (4 * nr * nc * 16) == 0 else 2
    half = rows // parts // 2
    rc = half // nr
    nz = nc // 2
    zc = rc // nz
    vmem = pl.BlockSpec(memory_space=pltpu.VMEM)
    slots = 2 * (1 + nr - 1 + nz - 1)
    tile = pltpu.VMEM(dmid.shape, BF)
    total, glat = pl.pallas_call(
        functools.partial(finish, cfg, parts),
        name="finish",
        out_shape=[jax.ShapeDtypeStruct((rows, width), BF), jax.ShapeDtypeStruct(dmid.shape, BF)],
        in_specs=[vmem] * 6,
        out_specs=[vmem] * 2,
        scratch_shapes=[
            pltpu.VMEM((rows // 2, width), BF),
        ] + [tile] * 13 + [
            pltpu.VMEM((parts, half, width), BF),
            pltpu.VMEM((parts, half, width), BF),
            pltpu.VMEM((parts, nr - 1, rc, width), BF),
            pltpu.VMEM((parts, rc, width), BF),
            pltpu.VMEM((parts, nz - 1, zc, width), BF),
            pltpu.SemaphoreType.DMA((parts, slots)),
            pltpu.SemaphoreType.DMA((parts, slots)),
            pltpu.SemaphoreType.DMA((2, nr - 1)),
            pltpu.SemaphoreType.DMA((2, nc - 1)),
            pltpu.SemaphoreType.DMA((2, nc - 1)),
        ],
        compiler_params=pltpu.CompilerParams(
            collective_id=0, has_side_effects=True, vmem_limit_bytes=36 * 2**20
        ),
        cost_estimate=pl.CostEstimate(flops=10**9, bytes_accessed=200 * 2**20, transcendentals=0),
    )(dmid, dw_col, w_row, gain_row, *saved)
    total = total.reshape((2,) + shape)
    return total[1].astype(F32), total[0].astype(F32), glat


def body(sizes, latents, cotangent, w_row, w_col, keep_heads):
    nr, nc = sizes
    rt, ct, width = latents.shape
    ri, cj = rt // nc, ct // nr
    cfg = (nr, nc, ri, cj)
    tokens = rt * ct
    flat = (tokens, width)
    gains = jnp.repeat(keep_heads.astype(F32), HEAD, axis=1)
    gain_row, gain_col = gains[:1], gains[1:]
    act = jax.ShapeDtypeStruct(flat, BF)
    dw = jax.ShapeDtypeStruct((w_row.shape[0] * width, width), BF)
    tile = pltpu.VMEM(flat, BF)
    vmem = pl.BlockSpec(memory_space=pltpu.VMEM)
    saved_u, saved_a, out, dmid, dw_col = pl.pallas_call(
        functools.partial(front, cfg),
        name="front",
        out_shape=[act, act, act, act, dw],
        in_specs=[vmem] * 6,
        out_specs=[vmem] * 5,
        scratch_shapes=[tile] * 18 + [
            pltpu.SemaphoreType.DMA((2, n - 1)) for n in (nc, nr, nc, nr)
        ],
        compiler_params=pltpu.CompilerParams(
            collective_id=1, has_side_effects=True, vmem_limit_bytes=36 * 2**20
        ),
        cost_estimate=pl.CostEstimate(
            flops=10**10, bytes_accessed=100 * 2**20, transcendentals=0
        ),
    )(latents.reshape(flat), cotangent.reshape(flat), w_row, gain_row, w_col, gain_col)
    saved = (saved_u, saved_a)
    pieces = out.reshape(nr, tokens // nr, width)
    output = lax.all_to_all(pieces, "row", split_axis=0, concat_axis=0, tiled=True)
    output = output.reshape(ct, rt, width).transpose(1, 0, 2)
    grad_row, grad_col, glat = last_kernel(cfg, dmid, dw_col, w_row, gain_row, saved)
    grad_latents = glat.reshape(latents.shape)
    return (output, grad_latents, grad_row, grad_col)


def solution(mesh):
    in_specs = (P("row", "col", None), P("row", "col", None), P(), P(), P())
    out_specs = (P("row", "col", None), P("row", "col", None), P(), P())
    sizes = (mesh.shape["row"], mesh.shape["col"])
    return jax.shard_map(
        functools.partial(body, sizes), mesh=mesh, in_specs=in_specs, out_specs=out_specs,
        check_vma=False,
    )
```
